512 devices in a mesh: ctx: 64 (over z, y_lo, core), chan: 8 (over x, y_hi).
Axes of the slice: x: 4, y: 4 (y_hi: 2, y_lo: 2; y = y_hi * 2 + y_lo), z: 16, core: 2. Of those that a mesh axis runs over, the one named last changes fastest.
Arguments:
- query_in: bfloat16 [8192, 1024], P('ctx', 'chan'), may hold values from -6 to 6
- key_in: bfloat16 [8192, 1024], P('ctx', 'chan'), may hold values from -6 to 6
- value_in: bfloat16 [8192, 1024], P('ctx', 'chan'), may hold values from -6 to 6
- grad_out: bfloat16 [8192, 1024], P('ctx', 'chan'), may hold values from -6 to 6
- residue: float32 [16, 1024], P(None, 'chan'), may hold values from -0.34 to 0.34
- decay_rate: float32 [16, 1024], P(None, 'chan'), may hold values from 1.0986328125e-05 to 0.05
Outputs:
- grad_query: bfloat16 [8192, 1024], P('ctx', 'chan')
- grad_key: bfloat16 [8192, 1024], P('ctx', 'chan')
- grad_value: bfloat16 [8192, 1024], P('ctx', 'chan')
- grad_residue: float32 [16, 1024], P(None, 'chan')
- grad_log_rate: float32 [16, 1024], P(None, 'chan')
- filter_norm: float32 [], replicated
The draws below stay inside these ranges and needn't reach their ends.
All inputs are finite; a program needn't handle non-finite values.
Results may differ from the reference program's by a relative error of at most 0.003.
Values may be sent and summed in bfloat16 or wider, within the bound.
No kernel may reach another device: no remote copies, remote signals or barrier semaphores. Data moves between devices by JAX's collectives and lax.ppermute only.
A program may use at most 64 MiB of HBM per device.

```python
import math
import jax
import jax.numpy as jnp
from jax import lax

CH = 1024
M = 16
SEQ = 8192


def rate_table(key, slow_share):
    picker = jax.random.uniform(jax.random.fold_in(key, 11), (M, CH), jnp.float32)
    slow_rates = jnp.exp(jax.random.uniform(jax.random.fold_in(key, 12), (M, CH), jnp.float32, math.log(0.1), math.log(2.0))) / SEQ
    fast_rates = jnp.exp(jax.random.uniform(jax.random.fold_in(key, 13), (M, CH), jnp.float32, math.log(0.02), math.log(0.05)))
    return jnp.where(picker < slow_share, slow_rates, fast_rates)


def draw_decay_rate(key, part):
    share = 0.5
    rates = rate_table(key, share)
    return rates.astype(jnp.float32)


def draw_residue(key, part):
    share = 0.5
    rates = rate_table(key, share)
    key = jax.random.fold_in(key, 5)
    noise = jax.random.truncated_normal(key, -4.0, 4.0, (M, CH), jnp.float32)
    return (noise * jnp.sqrt(2.0 * rates + 2.0 / SEQ) / math.sqrt(M)).astype(jnp.float32)


def level_of(stream_key, extent, shards, low, largest):
    def one(axis_at, blocks):
        draws = jax.random.uniform(jax.random.fold_in(jax.random.fold_in(stream_key, 6), axis_at), (blocks,), jnp.float32, low / len(shards), largest / len(shards))
        return jnp.repeat(jnp.exp(draws), extent[axis_at] // blocks).reshape((-1,) + (1,) * (len(extent) - axis_at - 1))

    gain = one(*shards[0])
    for cut in shards[1:]:
        gain = gain * one(*cut)
    return gain


def normal_values(stream_key, extent, width, bound, cuts=(), held_as=jnp.bfloat16):
    entries = jax.random.normal(stream_key, extent, jnp.float32) * width
    if len(cuts) > 0:
        entries = level_of(stream_key, extent, cuts, -0.22, 0.18) * entries
    return jnp.clip(entries, min=-bound, max=bound).astype(held_as)


def setup_inputs(seed: int = 0) -> dict:
    splits = jax.random.split(jax.random.key(seed), 7)
    query_in = normal_values(splits[0], (SEQ, CH), 1.0, 6.0, ((0, 64), (1, 8)))
    key_in = normal_values(splits[1], (SEQ, CH), 1.0, 6.0, ((0, 64), (1, 8)))
    value_in = normal_values(splits[2], (SEQ, CH), 1.0, 6.0, ((0, 64), (1, 8)))
    grad_out = normal_values(splits[3], (SEQ, CH), 1.0, 6.0, ((0, 64), (1, 8)))
    residue = draw_residue(jax.random.fold_in(splits[6], 71), 0)
    decay_rate = draw_decay_rate(jax.random.fold_in(splits[6], 71), 0)
    return {"query_in": query_in, "key_in": key_in, "value_in": value_in, "grad_out": grad_out, "residue": residue, "decay_rate": decay_rate}


def forward_combine(early, late):
    return (early[0] * late[0], late[0] * early[1] + late[1])

def backward_combine(right, left):
    right_a, right_b, right_g, right_p = right
    left_a, left_b, left_g, left_p = left
    return (left_a * right_a, left_a * right_b + left_b * right_a, left_a * right_g + left_g, left_a * right_p + left_b * right_g + left_p)

def channel_block(pieces):
    mixed_in, grad_mix, rates, residues = pieces
    row_count = mixed_in.shape[0]
    shape = (row_count,) + rates.shape
    factor = jnp.broadcast_to(jnp.exp(-rates), shape)
    source = jnp.broadcast_to(mixed_in[:, None, :], shape)
    _, states = lax.associative_scan(forward_combine, (factor, source), axis=0)
    conv = lax.optimization_barrier(jnp.sum(residues[None] * states, axis=1))
    target = jnp.broadcast_to(grad_mix[:, None, :], shape)
    _, _, adjoint, second = lax.associative_scan(backward_combine, (factor, factor, target, jnp.zeros(shape, jnp.float32)), axis=0, reverse=True)
    grad_conv = lax.optimization_barrier(jnp.sum(residues[None] * adjoint, axis=1))
    res_sum = lax.optimization_barrier(jnp.sum(mixed_in[:, None, :] * adjoint, axis=0))
    rate_sum = lax.optimization_barrier(jnp.sum(mixed_in[:, None, :] * second, axis=0))
    return (conv, grad_conv, res_sum, rate_sum)

def reference(query_in, key_in, value_in, grad_out, residue, decay_rate):
    mixed_in = key_in.astype(jnp.float32) * value_in.astype(jnp.float32)
    grad_mix = grad_out.astype(jnp.float32) * query_in.astype(jnp.float32)
    block_width = min(64, CH)
    block_count = CH // block_width
    mixed_t = mixed_in.reshape(SEQ, block_count, block_width).transpose(1, 0, 2)
    grad_t = grad_mix.reshape(SEQ, block_count, block_width).transpose(1, 0, 2)
    rate_t = decay_rate.reshape(M, block_count, block_width).transpose(1, 0, 2)
    res_t = residue.reshape(M, block_count, block_width).transpose(1, 0, 2)
    conv, grad_conv, res_sum, rate_sum = lax.map(channel_block, (mixed_t, grad_t, rate_t, res_t))
    conv = conv.transpose(1, 0, 2).reshape(SEQ, CH)
    grad_conv = grad_conv.transpose(1, 0, 2).reshape(SEQ, CH)
    res_sum = res_sum.transpose(1, 0, 2).reshape(M, CH)
    rate_sum = rate_sum.transpose(1, 0, 2).reshape(M, CH)
    grad_query = (grad_out.astype(jnp.float32) * conv).astype(jnp.bfloat16)
    grad_key = (grad_conv * value_in.astype(jnp.float32)).astype(jnp.bfloat16)
    grad_value = (grad_conv * key_in.astype(jnp.float32)).astype(jnp.bfloat16)
    grad_residue = res_sum / SEQ
    grad_log_rate = -decay_rate * residue * rate_sum / SEQ
    filter_norm = jnp.sqrt(jnp.sum(grad_residue * grad_residue + grad_log_rate * grad_log_rate))
    return (grad_query, grad_key, grad_value, grad_residue, grad_log_rate, filter_norm)
```

```python
import jax
import jax.numpy as jnp
from jax import lax
from jax.experimental import pallas as pl
from jax.experimental.pallas import tpu as pltpu
from jax.sharding import Mesh, PartitionSpec as P

ROWS = 128
LANES = 128
MODES = 16
GROUP = 4
NEAR = 2
RING = 8
BLOCKS = NEAR * GROUP
SHARE = MODES // GROUP
CHANS = 8
TOTAL = ROWS * BLOCKS * RING
F32 = jnp.float32
VM = pl.BlockSpec(memory_space=pltpu.VMEM)


def group_index():
    return lax.axis_index("yl") * 2 + lax.axis_index("core")


def summary_kernel(q_ref, k_ref, v_ref, g_ref, rate_ref, res_ref, out_ref, own_ref, x_s, g_s):
    x_s[...] = k_ref[...].astype(F32) * v_ref[...].astype(F32)
    g_s[...] = g_ref[...].astype(F32) * q_ref[...].astype(F32)
    f = jnp.exp(-rate_ref[...])
    zero = jnp.zeros((MODES, LANES), F32)
    state, moment, adj, sec, res_sum, rate_sum = zero, zero, zero, zero, zero, zero
    for i in range(ROWS):
        j = ROWS - 1 - i
        moment = f * (moment + state)
        state = f * state + x_s[i : i + 1, :]
        sec = f * (sec + adj)
        adj = f * adj + g_s[j : j + 1, :]
        x_j = x_s[j : j + 1, :]
        res_sum = res_sum + x_j * adj
        rate_sum = rate_sum + x_j * sec
    for near in range(NEAR):
        for peer in range(GROUP):
            for at, part in enumerate((state, moment, adj, sec, res_sum, rate_sum)):
                rows = slice(SHARE * at, SHARE * (at + 1))
                out_ref[near * GROUP + peer, rows, :] = part[SHARE * peer : SHARE * (peer + 1)]
    me = group_index()
    for at, ref in enumerate((rate_ref, res_ref)):
        mine = jnp.zeros((SHARE, LANES), F32)
        for peer in range(GROUP):
            mine = jnp.where(me == peer, ref[SHARE * peer : SHARE * (peer + 1), :], mine)
        own_ref[SHARE * at : SHARE * (at + 1), :] = mine


def parts_of(ref, at):
    return tuple(ref[at, SHARE * k : SHARE * (k + 1), :] for k in range(6))


def near_kernel(in_ref, own_ref, out_ref):
    rate = own_ref[0:SHARE, :]
    f = jnp.exp(-rate)
    span = jnp.exp(-rate * ROWS)
    blocks = [parts_of(in_ref, d) for d in range(BLOCKS)]
    state, moment, _, _, res_sum, rate_sum = blocks[0]
    for d in range(1, BLOCKS):
        moment = span * (moment + ROWS * state) + blocks[d][1]
        state = span * state + blocks[d][0]
        res_sum = res_sum + blocks[d][4]
        rate_sum = rate_sum + blocks[d][5]
    adj, sec = blocks[-1][2], blocks[-1][3]
    for d in range(BLOCKS - 2, -1, -1):
        held = f * blocks[d][0]
        held_moment = f * (blocks[d][1] + blocks[d][0])
        res_sum = res_sum + held * adj
        rate_sum = rate_sum + held_moment * adj + held * sec
        sec = span * (sec + ROWS * adj) + blocks[d][3]
        adj = span * adj + blocks[d][2]
    for at, part in enumerate((state, moment, adj, sec, res_sum, rate_sum)):
        for z in range(RING):
            out_ref[z, SHARE * at : SHARE * (at + 1), :] = part


def ring_kernel(ring_ref, in_ref, own_ref, out_ref):
    ring_me, near_me = lax.axis_index("far"), lax.axis_index("near")
    rate = own_ref[0:SHARE, :]
    res = own_ref[SHARE : 2 * SHARE, :]
    f = jnp.exp(-rate)
    span = jnp.exp(-rate * ROWS)
    reach = ROWS * BLOCKS
    long = jnp.exp(-rate * reach)
    zero = jnp.zeros((SHARE, LANES), F32)
    enter = zero
    for z in range(RING - 1):
        enter = jnp.where(z < ring_me, long * enter + ring_ref[z, 0:SHARE, :], enter)
    adj, sec, leave, res_sum, rate_sum = zero, zero, zero, zero, zero
    for z in range(RING - 1, -1, -1):
        state, moment, adj_z, sec_z, res_z, rate_z = parts_of(ring_ref, z)
        leave = jnp.where(z == ring_me, adj, leave)
        held = f * state
        held_moment = f * (moment + state)
        res_sum = res_sum + res_z + held * adj
        rate_sum = rate_sum + rate_z + held_moment * adj + held * sec
        sec = long * (sec + reach * adj) + sec_z
        adj = long * adj + adj_z
    grad_res = res_sum * (1.0 / TOTAL)
    grad_rate = -rate * res * rate_sum * (1.0 / TOTAL)
    enters, leaves = [enter], [leave]
    for d in range(BLOCKS - 1):
        enters.append(span * enters[-1] + in_ref[d, 0:SHARE, :])
        leaves.append(span * leaves[-1] + in_ref[BLOCKS - 1 - d, 2 * SHARE : 3 * SHARE, :])
    leaves = leaves[::-1]
    for d in range(GROUP):
        mine = [jnp.where(near_me == 0, many[d], many[GROUP + d]) for many in (enters, leaves)]
        for chan in range(CHANS):
            for at, part in enumerate((*mine, grad_res, grad_rate)):
                out_ref[chan * GROUP + d, SHARE * at : SHARE * (at + 1), :] = part


def final_kernel(
    back_ref, q_ref, k_ref, v_ref, g_ref, rate_ref, res_ref,
    gq_ref, gk_ref, gv_ref, gres_ref, grate_ref, norm_ref, x_s, g_s,
):
    first = (lax.axis_index("x") * 2 + lax.axis_index("yh")) * GROUP
    x_s[...] = k_ref[...].astype(F32) * v_ref[...].astype(F32)
    g_s[...] = g_ref[...].astype(F32) * q_ref[...].astype(F32)
    f = jnp.exp(-rate_ref[...])
    res = res_ref[...]

    def gathered(at):
        return jnp.concatenate([back_ref[first + d, SHARE * at : SHARE * (at + 1), :] for d in range(GROUP)], axis=0)

    squares = jnp.zeros((2 * SHARE, LANES), F32)
    for peer in range(CHANS * GROUP):
        part = back_ref[peer, 2 * SHARE : 4 * SHARE, :]
        squares = squares + part * part
    norm_ref[...] = jnp.sqrt(jnp.sum(squares, keepdims=True))
    gres_ref[...] = gathered(2)
    grate_ref[...] = gathered(3)
    state = gathered(0)
    adj = gathered(1)
    step = 16
    for base in range(0, ROWS, step):
        conv, grad = [], []
        for i in range(base, base + step):
            j = ROWS - 1 - i
            state = f * state + x_s[i : i + 1, :]
            adj = f * adj + g_s[j : j + 1, :]
            conv.append(jnp.sum(res * state, axis=0, keepdims=True))
            grad.append(jnp.sum(res * adj, axis=0, keepdims=True))
        conv = jnp.concatenate(conv, axis=0)
        grad = jnp.concatenate(grad[::-1], axis=0)
        rows = slice(base, base + step)
        gq_ref[rows, :] = (g_ref[rows, :].astype(F32) * conv).astype(jnp.bfloat16)
        rows = slice(ROWS - base - step, ROWS - base)
        gk_ref[rows, :] = (v_ref[rows, :].astype(F32) * grad).astype(jnp.bfloat16)
        gv_ref[rows, :] = (k_ref[rows, :].astype(F32) * grad).astype(jnp.bfloat16)


def call(kernel, shapes, scratch=(), vmem_in=True, vmem_out=True):
    run = pl.pallas_call(
        kernel,
        out_shape=[(pltpu.VMEM if vmem_out else jax.ShapeDtypeStruct)(s, t) for s, t in shapes],
        out_specs=[VM] * len(shapes),
        scratch_shapes=list(scratch),
    )
    if not vmem_in:
        return run
    return lambda *args: run(*[pltpu.with_memory_space_constraint(a, pltpu.VMEM) for a in args])


def on_device(query_in, key_in, value_in, grad_out, residue, decay_rate):
    block = pltpu.VMEM((ROWS, LANES), F32)
    summary, own = call(
        summary_kernel, [((BLOCKS, 6 * SHARE, LANES), F32), ((2 * SHARE, LANES), F32)], [block, block], vmem_in=False
    )(query_in, key_in, value_in, grad_out, decay_rate, residue)
    near = lax.all_to_all(summary, ("near", "yl", "core"), split_axis=0, concat_axis=0, tiled=True)
    (composite,) = call(near_kernel, [((RING, 6 * SHARE, LANES), F32)])(near, own)
    ring = lax.all_to_all(composite, "far", split_axis=0, concat_axis=0, tiled=True)
    (message,) = call(ring_kernel, [((CHANS * GROUP, 4 * SHARE, LANES), F32)])(ring, near, own)
    back = lax.all_to_all(message, ("x", "yh", "yl", "core"), split_axis=0, concat_axis=0, tiled=True)
    bf = jnp.bfloat16
    gq, gk, gv, gres, grate, norm = call(
        final_kernel,
        [((ROWS, LANES), bf)] * 3 + [((MODES, LANES), F32)] * 2 + [((1, 1), F32)],
        [block, block],
        vmem_out=False,
    )(back, query_in, key_in, value_in, grad_out, decay_rate, residue)
    return gq, gk, gv, gres, grate, norm.reshape(())


def solution(mesh):
    fine = Mesh(mesh.devices.reshape(RING, NEAR, 2, 2, 4, 2), ("far", "near", "yl", "core", "x", "yh"))
    ctx, chan = ("far", "near", "yl", "core"), ("x", "yh")
    return jax.shard_map(
        on_device,
        mesh=fine,
        in_specs=(P(ctx, chan),) * 4 + (P(None, chan),) * 2,
        out_specs=(P(ctx, chan),) * 3 + (P(None, chan),) * 2 + (P(),),
        check_vma=False,
    )
```

```python
import jax
import jax.numpy as jnp
from jax import lax
from jax.experimental import pallas as pl
from jax.experimental.pallas import tpu as pltpu
from jax.sharding import Mesh, PartitionSpec as P

ROWS = 128
LANES = 128
MODES = 16
GROUP = 4
NEAR = 2
RING = 8
BLOCKS = NEAR * GROUP
SHARE = MODES // GROUP
CHANS = 8
NEAR_FIRST = 4
RING_FIRST = 4
PLANE_FIRST = 20
TOTAL = ROWS * BLOCKS * RING
F32 = jnp.float32
VM = pl.BlockSpec(memory_space=pltpu.VMEM)


def group_index():
    return lax.axis_index("yl") * 2 + lax.axis_index("core")


def summary_kernel(q_ref, k_ref, v_ref, g_ref, rate_ref, res_ref, out_ref, own_ref, x_s, g_s):
    x_s[...] = k_ref[...].astype(F32) * v_ref[...].astype(F32)
    g_s[...] = g_ref[...].astype(F32) * q_ref[...].astype(F32)
    f = jnp.exp(-rate_ref[...])
    zero = jnp.zeros((MODES, LANES), F32)
    state, moment, adj, sec, res_sum, rate_sum = zero, zero, zero, zero, zero, zero
    for i in range(ROWS):
        j = ROWS - 1 - i
        moment = f * (moment + state)
        state = f * state + x_s[i : i + 1, :]
        sec = f * (sec + adj)
        adj = f * adj + g_s[j : j + 1, :]
        x_j = x_s[j : j + 1, :]
        res_sum = res_sum + x_j * adj
        rate_sum = rate_sum + x_j * sec
    for near in range(NEAR):
        for peer in range(GROUP):
            for at, part in enumerate((state, moment, adj, sec, res_sum, rate_sum)):
                rows = slice(SHARE * at, SHARE * (at + 1))
                out_ref[(near * GROUP + peer) ^ NEAR_FIRST, rows, :] = part[SHARE * peer : SHARE * (peer + 1)]
    me = group_index()
    for at, ref in enumerate((rate_ref, res_ref)):
        mine = jnp.zeros((SHARE, LANES), F32)
        for peer in range(GROUP):
            mine = jnp.where(me == peer, ref[SHARE * peer : SHARE * (peer + 1), :], mine)
        own_ref[SHARE * at : SHARE * (at + 1), :] = mine


def parts_of(ref, at):
    return tuple(ref[at, SHARE * k : SHARE * (k + 1), :] for k in range(6))


def near_kernel(in_ref, own_ref, out_ref):
    rate = own_ref[0:SHARE, :]
    f = jnp.exp(-rate)
    span = jnp.exp(-rate * ROWS)
    blocks = [parts_of(in_ref, d ^ NEAR_FIRST) for d in range(BLOCKS)]
    state, moment, _, _, res_sum, rate_sum = blocks[0]
    for d in range(1, BLOCKS):
        moment = span * (moment + ROWS * state) + blocks[d][1]
        state = span * state + blocks[d][0]
        res_sum = res_sum + blocks[d][4]
        rate_sum = rate_sum + blocks[d][5]
    adj, sec = blocks[-1][2], blocks[-1][3]
    for d in range(BLOCKS - 2, -1, -1):
        held = f * blocks[d][0]
        held_moment = f * (blocks[d][1] + blocks[d][0])
        res_sum = res_sum + held * adj
        rate_sum = rate_sum + held_moment * adj + held * sec
        sec = span * (sec + ROWS * adj) + blocks[d][3]
        adj = span * adj + blocks[d][2]
    for at, part in enumerate((state, moment, adj, sec, res_sum, rate_sum)):
        for z in range(RING):
            out_ref[z, SHARE * at : SHARE * (at + 1), :] = part


def ring_kernel(ring_ref, in_ref, own_ref, out_ref):
    ring_me, near_me = lax.axis_index("far"), lax.axis_index("near")
    rate = own_ref[0:SHARE, :]
    res = own_ref[SHARE : 2 * SHARE, :]
    f = jnp.exp(-rate)
    span = jnp.exp(-rate * ROWS)
    reach = ROWS * BLOCKS
    long = jnp.exp(-rate * reach)
    zero = jnp.zeros((SHARE, LANES), F32)
    enter = zero
    for z in range(RING - 1):
        enter = jnp.where(z < ring_me, long * enter + ring_ref[z ^ RING_FIRST, 0:SHARE, :], enter)
    adj, sec, leave, res_sum, rate_sum = zero, zero, zero, zero, zero
    for z in range(RING - 1, -1, -1):
        state, moment, adj_z, sec_z, res_z, rate_z = parts_of(ring_ref, z ^ RING_FIRST)
        leave = jnp.where(z == ring_me, adj, leave)
        held = f * state
        held_moment = f * (moment + state)
        res_sum = res_sum + res_z + held * adj
        rate_sum = rate_sum + rate_z + held_moment * adj + held * sec
        sec = long * (sec + reach * adj) + sec_z
        adj = long * adj + adj_z
    grad_res = res_sum * (1.0 / TOTAL)
    grad_rate = -rate * res * rate_sum * (1.0 / TOTAL)
    enters, leaves = [enter], [leave]
    for d in range(BLOCKS - 1):
        enters.append(span * enters[-1] + in_ref[d ^ NEAR_FIRST, 0:SHARE, :])
        leaves.append(span * leaves[-1] + in_ref[(BLOCKS - 1 - d) ^ NEAR_FIRST, 2 * SHARE : 3 * SHARE, :])
    leaves = leaves[::-1]
    for d in range(GROUP):
        mine = [jnp.where(near_me == 0, many[d], many[GROUP + d]) for many in (enters, leaves)]
        for chan in range(CHANS):
            for at, part in enumerate((*mine, grad_res, grad_rate)):
                out_ref[(chan * GROUP + d) ^ PLANE_FIRST, SHARE * at : SHARE * (at + 1), :] = part


def final_kernel(
    back_ref, q_ref, k_ref, v_ref, g_ref, rate_ref, res_ref,
    gq_ref, gk_ref, gv_ref, gres_ref, grate_ref, norm_ref, x_s, g_s,
):
    first = ((lax.axis_index("x") * 2 + lax.axis_index("yh")) ^ (PLANE_FIRST // GROUP)) * GROUP
    x_s[...] = k_ref[...].astype(F32) * v_ref[...].astype(F32)
    g_s[...] = g_ref[...].astype(F32) * q_ref[...].astype(F32)
    f = jnp.exp(-rate_ref[...])
    res = res_ref[...]

    def gathered(at):
        return jnp.concatenate([back_ref[first + (d ^ (PLANE_FIRST % GROUP)), SHARE * at : SHARE * (at + 1), :] for d in range(GROUP)], axis=0)

    squares = jnp.zeros((2 * SHARE, LANES), F32)
    for peer in range(CHANS * GROUP):
        part = back_ref[peer, 2 * SHARE : 4 * SHARE, :]
        squares = squares + part * part
    norm_ref[...] = jnp.sqrt(jnp.sum(squares, keepdims=True))
    gres_ref[...] = gathered(2)
    grate_ref[...] = gathered(3)
    state = gathered(0)
    adj = gathered(1)
    step = 16
    for base in range(0, ROWS, step):
        conv, grad = [], []
        for i in range(base, base + step):
            j = ROWS - 1 - i
            state = f * state + x_s[i : i + 1, :]
            adj = f * adj + g_s[j : j + 1, :]
            conv.append(jnp.sum(res * state, axis=0, keepdims=True))
            grad.append(jnp.sum(res * adj, axis=0, keepdims=True))
        conv = jnp.concatenate(conv, axis=0)
        grad = jnp.concatenate(grad[::-1], axis=0)
        rows = slice(base, base + step)
        gq_ref[rows, :] = (g_ref[rows, :].astype(F32) * conv).astype(jnp.bfloat16)
        rows = slice(ROWS - base - step, ROWS - base)
        gk_ref[rows, :] = (v_ref[rows, :].astype(F32) * grad).astype(jnp.bfloat16)
        gv_ref[rows, :] = (k_ref[rows, :].astype(F32) * grad).astype(jnp.bfloat16)


def call(kernel, shapes, scratch=(), vmem_in=True, vmem_out=True):
    run = pl.pallas_call(
        kernel,
        out_shape=[(pltpu.VMEM if vmem_out else jax.ShapeDtypeStruct)(s, t) for s, t in shapes],
        out_specs=[VM] * len(shapes),
        scratch_shapes=list(scratch),
    )
    if not vmem_in:
        return run
    return lambda *args: run(*[pltpu.with_memory_space_constraint(a, pltpu.VMEM) for a in args])


def exchange(blocks, axes, first):
    order = [p ^ first for p in range(blocks.shape[0])]
    return lax.all_to_all(blocks, axes, split_axis=0, concat_axis=0, axis_index_groups=[order], tiled=True)


def on_device(query_in, key_in, value_in, grad_out, residue, decay_rate):
    block = pltpu.VMEM((ROWS, LANES), F32)
    summary, own = call(
        summary_kernel, [((BLOCKS, 6 * SHARE, LANES), F32), ((2 * SHARE, LANES), F32)], [block, block], vmem_in=False
    )(query_in, key_in, value_in, grad_out, decay_rate, residue)
    near = exchange(summary, ("near", "yl", "core"), NEAR_FIRST)
    (composite,) = call(near_kernel, [((RING, 6 * SHARE, LANES), F32)])(near, own)
    ring = exchange(composite, "far", RING_FIRST)
    (message,) = call(ring_kernel, [((CHANS * GROUP, 4 * SHARE, LANES), F32)])(ring, near, own)
    back = exchange(message, ("x", "yh", "yl", "core"), PLANE_FIRST)
    bf = jnp.bfloat16
    gq, gk, gv, gres, grate, norm = call(
        final_kernel,
        [((ROWS, LANES), bf)] * 3 + [((MODES, LANES), F32)] * 2 + [((1, 1), F32)],
        [block, block],
        vmem_out=False,
    )(back, query_in, key_in, value_in, grad_out, decay_rate, residue)
    return gq, gk, gv, gres, grate, norm.reshape(())


def solution(mesh):
    fine = Mesh(mesh.devices.reshape(RING, NEAR, 2, 2, 4, 2), ("far", "near", "yl", "core", "x", "yh"))
    ctx, chan = ("far", "near", "yl", "core"), ("x", "yh")
    return jax.shard_map(
        on_device,
        mesh=fine,
        in_specs=(P(ctx, chan),) * 4 + (P(None, chan),) * 2,
        out_specs=(P(ctx, chan),) * 3 + (P(None, chan),) * 2 + (P(),),
        check_vma=False,
    )
```

```python
import jax
import jax.numpy as jnp
from jax import lax
from jax.experimental import pallas as pl
from jax.experimental.pallas import tpu as pltpu
from jax.sharding import Mesh, PartitionSpec as P

ROWS = 128
LANES = 128
MODES = 16
GROUP = 4
NEAR = 2
RING = 8
BLOCKS = NEAR * GROUP
SHARE = MODES // GROUP
CHANS = 8
NEAR_FIRST = 4
RING_ORDER = (4, 0, 5, 1, 6, 2, 7, 3)
PLANE_FIRST = 20
TOTAL = ROWS * BLOCKS * RING
F32 = jnp.float32
TINY = 1e-37
RING_CODES = ((256.0, 1), (8.0, 1), (256.0, 1), (8.0, 1), (256.0, 2), (64.0, 2))
CARRY_CODE = (64.0, 1)
GRAD_CODE = (1024.0, 2)
VM = pl.BlockSpec(memory_space=pltpu.VMEM)


def group_index():
    return lax.axis_index("yl") * 2 + lax.axis_index("core")


def summary_kernel(
    q_ref, k_ref, v_ref, g_ref, rate_ref, res_ref,
    out_ref, own_ref, x_s, g_s, k_keep, v_keep, g_keep, rate_keep, res_keep,
):
    x_s[...] = k_ref[...].astype(F32) * v_ref[...].astype(F32)
    g_s[...] = g_ref[...].astype(F32) * q_ref[...].astype(F32)
    kept = ((k_keep, k_ref), (v_keep, v_ref), (g_keep, g_ref), (rate_keep, rate_ref), (res_keep, res_ref))
    for keep, ref in kept:
        keep[...] = ref[...]
    f = jnp.exp(-rate_ref[...])
    zero = jnp.zeros((MODES, LANES), F32)
    state, moment, adj, sec, res_sum, rate_sum = zero, zero, zero, zero, zero, zero
    for i in range(ROWS):
        j = ROWS - 1 - i
        moment = f * (moment + state)
        state = f * state + x_s[i : i + 1, :]
        sec = f * (sec + adj)
        adj = f * adj + g_s[j : j + 1, :]
        x_j = x_s[j : j + 1, :]
        res_sum = res_sum + x_j * adj
        rate_sum = rate_sum + x_j * sec
    for near in range(NEAR):
        for peer in range(GROUP):
            for at, part in enumerate((state, moment, adj, sec, res_sum, rate_sum)):
                rows = slice(SHARE * at, SHARE * (at + 1))
                out_ref[(near * GROUP + peer) ^ NEAR_FIRST, rows, :] = part[SHARE * peer : SHARE * (peer + 1)]
    me = group_index()
    for at, ref in enumerate((rate_ref, res_ref)):
        mine = jnp.zeros((SHARE, LANES), F32)
        for peer in range(GROUP):
            mine = jnp.where(me == peer, ref[SHARE * peer : SHARE * (peer + 1), :], mine)
        own_ref[SHARE * at : SHARE * (at + 1), :] = mine


def rooted(v):
    return v * lax.rsqrt(jnp.abs(v) + TINY)


def coded(v, gain, roots):
    for _ in range(roots):
        v = rooted(v)
    return v * gain


def decoded(y, gain, roots):
    y = y * (1.0 / gain)
    for _ in range(roots):
        y = y * jnp.abs(y)
    return y


def parts_of(ref, at, codes=None):
    parts = tuple(ref[at, SHARE * k : SHARE * (k + 1), :] for k in range(6))
    return parts if codes is None else tuple(decoded(p, *c) for p, c in zip(parts, codes))


def near_kernel(in_ref, own_ref, out_ref):
    rate = own_ref[0:SHARE, :]
    f = jnp.exp(-rate)
    span = jnp.exp(-rate * ROWS)
    blocks = [parts_of(in_ref, d ^ NEAR_FIRST) for d in range(BLOCKS)]
    state, moment, _, _, res_sum, rate_sum = blocks[0]
    for d in range(1, BLOCKS):
        moment = span * (moment + ROWS * state) + blocks[d][1]
        state = span * state + blocks[d][0]
        res_sum = res_sum + blocks[d][4]
        rate_sum = rate_sum + blocks[d][5]
    adj, sec = blocks[-1][2], blocks[-1][3]
    for d in range(BLOCKS - 2, -1, -1):
        held = f * blocks[d][0]
        held_moment = f * (blocks[d][1] + blocks[d][0])
        res_sum = res_sum + held * adj
        rate_sum = rate_sum + held_moment * adj + held * sec
        sec = span * (sec + ROWS * adj) + blocks[d][3]
        adj = span * adj + blocks[d][2]
    for at, part in enumerate((state, moment, adj, sec, res_sum, rate_sum)):
        part = coded(part, *RING_CODES[at])
        for z in range(RING):
            out_ref[z, SHARE * at : SHARE * (at + 1), :] = part


def ring_kernel(ring_ref, in_ref, own_ref, out_ref):
    ring_me, near_me = lax.axis_index("far"), lax.axis_index("near")
    rate = own_ref[0:SHARE, :]
    res = own_ref[SHARE : 2 * SHARE, :]
    f = jnp.exp(-rate)
    span = jnp.exp(-rate * ROWS)
    reach = ROWS * BLOCKS
    long = jnp.exp(-rate * reach)
    zero = jnp.zeros((SHARE, LANES), F32)
    composites = [parts_of(ring_ref, RING_ORDER.index(z), RING_CODES) for z in range(RING)]
    enter = zero
    for z in range(RING - 1):
        enter = jnp.where(z < ring_me, long * enter + composites[z][0], enter)
    adj, sec, leave, res_sum, rate_sum = zero, zero, zero, zero, zero
    for z in range(RING - 1, -1, -1):
        state, moment, adj_z, sec_z, res_z, rate_z = composites[z]
        leave = jnp.where(z == ring_me, adj, leave)
        held = f * state
        held_moment = f * (moment + state)
        res_sum = res_sum + res_z + held * adj
        rate_sum = rate_sum + rate_z + held_moment * adj + held * sec
        sec = long * (sec + reach * adj) + sec_z
        adj = long * adj + adj_z
    grad_res = res_sum * (1.0 / TOTAL)
    grad_rate = -rate * res * rate_sum * (1.0 / TOTAL)
    enters, leaves = [enter], [leave]
    for d in range(BLOCKS - 1):
        enters.append(span * enters[-1] + in_ref[d ^ NEAR_FIRST, 0:SHARE, :])
        leaves.append(span * leaves[-1] + in_ref[(BLOCKS - 1 - d) ^ NEAR_FIRST, 2 * SHARE : 3 * SHARE, :])
    leaves = leaves[::-1]
    for d in range(GROUP):
        mine = [jnp.where(near_me == 0, many[d], many[GROUP + d]) for many in (enters, leaves)]
        parts = [coded(p, *CARRY_CODE) for p in mine] + [coded(p, *GRAD_CODE) for p in (grad_res, grad_rate)]
        for chan in range(CHANS):
            for at, part in enumerate(parts):
                out_ref[(chan * GROUP + d) ^ PLANE_FIRST, SHARE * at : SHARE * (at + 1), :] = part


def final_kernel(
    back_ref, x_s, g_s, k_ref, v_ref, g_ref, rate_ref, res_ref,
    gq_ref, gk_ref, gv_ref, gres_ref, grate_ref, norm_ref,
):
    first = ((lax.axis_index("x") * 2 + lax.axis_index("yh")) ^ (PLANE_FIRST // GROUP)) * GROUP
    f = jnp.exp(-rate_ref[...])
    res = res_ref[...]

    def gathered(at, code):
        rows = slice(SHARE * at, SHARE * (at + 1))
        parts = [back_ref[first + (d ^ (PLANE_FIRST % GROUP)), rows, :] for d in range(GROUP)]
        return decoded(jnp.concatenate(parts, axis=0), *code)

    squares = jnp.zeros((2 * SHARE, LANES), F32)
    for peer in range(CHANS * GROUP):
        part = decoded(back_ref[peer, 2 * SHARE : 4 * SHARE, :], *GRAD_CODE)
        squares = squares + part * part
    norm_ref[...] = jnp.sqrt(jnp.sum(squares, keepdims=True))
    gres_ref[...] = gathered(2, GRAD_CODE)
    grate_ref[...] = gathered(3, GRAD_CODE)
    state = gathered(0, CARRY_CODE)
    adj = gathered(1, CARRY_CODE)
    step = 16
    for base in range(0, ROWS, step):
        conv, grad = [], []
        for i in range(base, base + step):
            j = ROWS - 1 - i
            state = f * state + x_s[i : i + 1, :]
            adj = f * adj + g_s[j : j + 1, :]
            conv.append(jnp.sum(res * state, axis=0, keepdims=True))
            grad.append(jnp.sum(res * adj, axis=0, keepdims=True))
        conv = jnp.concatenate(conv, axis=0)
        grad = jnp.concatenate(grad[::-1], axis=0)
        rows = slice(base, base + step)
        gq_ref[rows, :] = (g_ref[rows, :].astype(F32) * conv).astype(jnp.bfloat16)
        rows = slice(ROWS - base - step, ROWS - base)
        gk_ref[rows, :] = (v_ref[rows, :].astype(F32) * grad).astype(jnp.bfloat16)
        gv_ref[rows, :] = (k_ref[rows, :].astype(F32) * grad).astype(jnp.bfloat16)


def call(kernel, shapes, scratch=(), vmem_in=True, vmem_out=True):
    run = pl.pallas_call(
        kernel,
        out_shape=[(pltpu.VMEM if vmem_out else jax.ShapeDtypeStruct)(s, t) for s, t in shapes],
        out_specs=[VM] * len(shapes),
        scratch_shapes=list(scratch),
    )
    if not vmem_in:
        return run
    return lambda *args: run(*[pltpu.with_memory_space_constraint(a, pltpu.VMEM) for a in args])


def exchange(blocks, axes, order):
    return lax.all_to_all(blocks, axes, split_axis=0, concat_axis=0, axis_index_groups=[list(order)], tiled=True)


def on_device(query_in, key_in, value_in, grad_out, residue, decay_rate):
    bf = jnp.bfloat16
    block, table = (ROWS, LANES), (MODES, LANES)
    summary, own, *kept = call(
        summary_kernel,
        [((BLOCKS, 6 * SHARE, LANES), F32), ((2 * SHARE, LANES), F32)]
        + [(block, F32)] * 2 + [(block, bf)] * 3 + [(table, F32)] * 2,
        vmem_in=False,
    )(query_in, key_in, value_in, grad_out, decay_rate, residue)
    near = exchange(summary, ("near", "yl", "core"), [p ^ NEAR_FIRST for p in range(BLOCKS)])
    (composite,) = call(near_kernel, [((RING, 6 * SHARE, LANES), F32)])(near, own)
    ring = exchange(composite.astype(jnp.float16), "far", RING_ORDER).astype(F32)
    (message,) = call(ring_kernel, [((CHANS * GROUP, 4 * SHARE, LANES), F32)])(ring, near, own)
    order = [p ^ PLANE_FIRST for p in range(CHANS * GROUP)]
    back = exchange(message.astype(jnp.float16), ("x", "yh", "yl", "core"), order).astype(F32)
    gq, gk, gv, gres, grate, norm = call(
        final_kernel, [(block, bf)] * 3 + [(table, F32)] * 2 + [((1, 1), F32)], vmem_out=False
    )(back, *kept)
    return gq, gk, gv, gres, grate, norm.reshape(())


def solution(mesh):
    fine = Mesh(mesh.devices.reshape(RING, NEAR, 2, 2, 4, 2), ("far", "near", "yl", "core", "x", "yh"))
    ctx, chan = ("far", "near", "yl", "core"), ("x", "yh")
    return jax.shard_map(
        on_device,
        mesh=fine,
        in_specs=(P(ctx, chan),) * 4 + (P(None, chan),) * 2,
        out_specs=(P(ctx, chan),) * 3 + (P(None, chan),) * 2 + (P(),),
        check_vma=False,
    )
```

```python
import jax
import jax.numpy as jnp
from jax import lax
from jax.experimental import pallas as pl
from jax.experimental.pallas import tpu as pltpu
from jax.sharding import Mesh, PartitionSpec as P

ROWS = 128
LANES = 128
MODES = 16
GROUP = 4
NEAR = 2
RING = 8
BLOCKS = NEAR * GROUP
SHARE = MODES // GROUP
CHANS = 8
NEAR_FIRST = 5
RING_ORDER = (4, 0, 5, 1, 6, 2, 7, 3)
PLANE_FIRST = 21
TOTAL = ROWS * BLOCKS * RING
F32 = jnp.float32
TINY = 1e-37
RING_CODES = ((256.0, 1), (8.0, 1), (256.0, 1), (8.0, 1), (256.0, 2), (64.0, 2))
CARRY_CODE = (64.0, 1)
GRAD_CODE = (1024.0, 2)
VM = pl.BlockSpec(memory_space=pltpu.VMEM)


def group_index():
    return lax.axis_index("yl") * 2 + lax.axis_index("core")


def summary_kernel(
    q_ref, k_ref, v_ref, g_ref, rate_ref, res_ref,
    out_ref, own_ref, x_s, g_s, k_keep, v_keep, g_keep, rate_keep, res_keep,
):
    x_s[...] = k_ref[...].astype(F32) * v_ref[...].astype(F32)
    g_s[...] = g_ref[...].astype(F32) * q_ref[...].astype(F32)
    kept = ((k_keep, k_ref), (v_keep, v_ref), (g_keep, g_ref), (rate_keep, rate_ref), (res_keep, res_ref))
    for keep, ref in kept:
        keep[...] = ref[...]
    f = jnp.exp(-rate_ref[...])
    zero = jnp.zeros((MODES, LANES), F32)
    state, moment, adj, sec, res_sum, rate_sum = zero, zero, zero, zero, zero, zero
    for i in range(ROWS):
        j = ROWS - 1 - i
        moment = f * (moment + state)
        state = f * state + x_s[i : i + 1, :]
        sec = f * (sec + adj)
        adj = f * adj + g_s[j : j + 1, :]
        x_j = x_s[j : j + 1, :]
        res_sum = res_sum + x_j * adj
        rate_sum = rate_sum + x_j * sec
    for near in range(NEAR):
        for peer in range(GROUP):
            for at, part in enumerate((state, moment, adj, sec, res_sum, rate_sum)):
                rows = slice(SHARE * at, SHARE * (at + 1))
                out_ref[(near * GROUP + peer) ^ NEAR_FIRST, rows, :] = part[SHARE * peer : SHARE * (peer + 1)]
    me = group_index()
    for at, ref in enumerate((rate_ref, res_ref)):
        mine = jnp.zeros((SHARE, LANES), F32)
        for peer in range(GROUP):
            mine = jnp.where(me == peer, ref[SHARE * peer : SHARE * (peer + 1), :], mine)
        own_ref[SHARE * at : SHARE * (at + 1), :] = mine


def rooted(v):
    return v * lax.rsqrt(jnp.abs(v) + TINY)


def coded(v, gain, roots):
    for _ in range(roots):
        v = rooted(v)
    return v * gain


def decoded(y, gain, roots):
    y = y * (1.0 / gain)
    for _ in range(roots):
        y = y * jnp.abs(y)
    return y


def parts_of(ref, at, codes=None):
    parts = tuple(ref[at, SHARE * k : SHARE * (k + 1), :] for k in range(6))
    return parts if codes is None else tuple(decoded(p, *c) for p, c in zip(parts, codes))


def near_kernel(in_ref, own_ref, out_ref):
    rate = own_ref[0:SHARE, :]
    f = jnp.exp(-rate)
    span = jnp.exp(-rate * ROWS)
    blocks = [parts_of(in_ref, d ^ NEAR_FIRST) for d in range(BLOCKS)]
    state, moment, _, _, res_sum, rate_sum = blocks[0]
    for d in range(1, BLOCKS):
        moment = span * (moment + ROWS * state) + blocks[d][1]
        state = span * state + blocks[d][0]
        res_sum = res_sum + blocks[d][4]
        rate_sum = rate_sum + blocks[d][5]
    adj, sec = blocks[-1][2], blocks[-1][3]
    for d in range(BLOCKS - 2, -1, -1):
        held = f * blocks[d][0]
        held_moment = f * (blocks[d][1] + blocks[d][0])
        res_sum = res_sum + held * adj
        rate_sum = rate_sum + held_moment * adj + held * sec
        sec = span * (sec + ROWS * adj) + blocks[d][3]
        adj = span * adj + blocks[d][2]
    for at, part in enumerate((state, moment, adj, sec, res_sum, rate_sum)):
        part = coded(part, *RING_CODES[at])
        for z in range(RING):
            out_ref[z, SHARE * at : SHARE * (at + 1), :] = part


def ring_kernel(ring_ref, in_ref, own_ref, out_ref):
    ring_me, near_me = lax.axis_index("far"), lax.axis_index("near")
    rate = own_ref[0:SHARE, :]
    res = own_ref[SHARE : 2 * SHARE, :]
    f = jnp.exp(-rate)
    span = jnp.exp(-rate * ROWS)
    reach = ROWS * BLOCKS
    long = jnp.exp(-rate * reach)
    zero = jnp.zeros((SHARE, LANES), F32)
    composites = [parts_of(ring_ref, RING_ORDER.index(z), RING_CODES) for z in range(RING)]
    enter = zero
    for z in range(RING - 1):
        enter = jnp.where(z < ring_me, long * enter + composites[z][0], enter)
    adj, sec, leave, res_sum, rate_sum = zero, zero, zero, zero, zero
    for z in range(RING - 1, -1, -1):
        state, moment, adj_z, sec_z, res_z, rate_z = composites[z]
        leave = jnp.where(z == ring_me, adj, leave)
        held = f * state
        held_moment = f * (moment + state)
        res_sum = res_sum + res_z + held * adj
        rate_sum = rate_sum + rate_z + held_moment * adj + held * sec
        sec = long * (sec + reach * adj) + sec_z
        adj = long * adj + adj_z
    grad_res = res_sum * (1.0 / TOTAL)
    grad_rate = -rate * res * rate_sum * (1.0 / TOTAL)
    enters, leaves = [enter], [leave]
    for d in range(BLOCKS - 1):
        enters.append(span * enters[-1] + in_ref[d ^ NEAR_FIRST, 0:SHARE, :])
        leaves.append(span * leaves[-1] + in_ref[(BLOCKS - 1 - d) ^ NEAR_FIRST, 2 * SHARE : 3 * SHARE, :])
    leaves = leaves[::-1]
    for d in range(GROUP):
        mine = [jnp.where(near_me == 0, many[d], many[GROUP + d]) for many in (enters, leaves)]
        parts = [coded(p, *CARRY_CODE) for p in mine] + [coded(p, *GRAD_CODE) for p in (grad_res, grad_rate)]
        for chan in range(CHANS):
            for at, part in enumerate(parts):
                out_ref[(chan * GROUP + d) ^ PLANE_FIRST, SHARE * at : SHARE * (at + 1), :] = part


def final_kernel(
    back_ref, x_s, g_s, k_ref, v_ref, g_ref, rate_ref, res_ref,
    gq_ref, gk_ref, gv_ref, gres_ref, grate_ref, norm_ref,
):
    first = ((lax.axis_index("x") * 2 + lax.axis_index("yh")) ^ (PLANE_FIRST // GROUP)) * GROUP
    f = jnp.exp(-rate_ref[...])
    res = res_ref[...]

    def gathered(at, code):
        rows = slice(SHARE * at, SHARE * (at + 1))
        parts = [back_ref[first + (d ^ (PLANE_FIRST % GROUP)), rows, :] for d in range(GROUP)]
        return decoded(jnp.concatenate(parts, axis=0), *code)

    squares = jnp.zeros((2 * SHARE, LANES), F32)
    for peer in range(CHANS * GROUP):
        part = decoded(back_ref[peer, 2 * SHARE : 4 * SHARE, :], *GRAD_CODE)
        squares = squares + part * part
    norm_ref[...] = jnp.sqrt(jnp.sum(squares, keepdims=True))
    gres_ref[...] = gathered(2, GRAD_CODE)
    grate_ref[...] = gathered(3, GRAD_CODE)
    state = gathered(0, CARRY_CODE)
    adj = gathered(1, CARRY_CODE)
    step = 16
    for base in range(0, ROWS, step):
        conv, grad = [], []
        for i in range(base, base + step):
            j = ROWS - 1 - i
            state = f * state + x_s[i : i + 1, :]
            adj = f * adj + g_s[j : j + 1, :]
            conv.append(jnp.sum(res * state, axis=0, keepdims=True))
            grad.append(jnp.sum(res * adj, axis=0, keepdims=True))
        conv = jnp.concatenate(conv, axis=0)
        grad = jnp.concatenate(grad[::-1], axis=0)
        rows = slice(base, base + step)
        gq_ref[rows, :] = (g_ref[rows, :].astype(F32) * conv).astype(jnp.bfloat16)
        rows = slice(ROWS - base - step, ROWS - base)
        gk_ref[rows, :] = (v_ref[rows, :].astype(F32) * grad).astype(jnp.bfloat16)
        gv_ref[rows, :] = (k_ref[rows, :].astype(F32) * grad).astype(jnp.bfloat16)


def call(kernel, shapes, scratch=(), vmem_in=True, vmem_out=True):
    run = pl.pallas_call(
        kernel,
        out_shape=[(pltpu.VMEM if vmem_out else jax.ShapeDtypeStruct)(s, t) for s, t in shapes],
        out_specs=[VM] * len(shapes),
        scratch_shapes=list(scratch),
    )
    if not vmem_in:
        return run
    return lambda *args: run(*[pltpu.with_memory_space_constraint(a, pltpu.VMEM) for a in args])


def exchange(blocks, axes, order):
    return lax.all_to_all(blocks, axes, split_axis=0, concat_axis=0, axis_index_groups=[list(order)], tiled=True)


def on_device(query_in, key_in, value_in, grad_out, residue, decay_rate):
    bf = jnp.bfloat16
    block, table = (ROWS, LANES), (MODES, LANES)
    summary, own, *kept = call(
        summary_kernel,
        [((BLOCKS, 6 * SHARE, LANES), F32), ((2 * SHARE, LANES), F32)]
        + [(block, F32)] * 2 + [(block, bf)] * 3 + [(table, F32)] * 2,
        vmem_in=False,
    )(query_in, key_in, value_in, grad_out, decay_rate, residue)
    near = exchange(summary, ("near", "yl", "core"), [p ^ NEAR_FIRST for p in range(BLOCKS)])
    (composite,) = call(near_kernel, [((RING, 6 * SHARE, LANES), F32)])(near, own)
    ring = exchange(composite.astype(jnp.float16), "far", RING_ORDER).astype(F32)
    (message,) = call(ring_kernel, [((CHANS * GROUP, 4 * SHARE, LANES), F32)])(ring, near, own)
    order = [p ^ PLANE_FIRST for p in range(CHANS * GROUP)]
    back = exchange(message.astype(jnp.float16), ("x", "yh", "yl", "core"), order).astype(F32)
    gq, gk, gv, gres, grate, norm = call(
        final_kernel, [(block, bf)] * 3 + [(table, F32)] * 2 + [((1, 1), F32)], vmem_out=False
    )(back, *kept)
    return gq, gk, gv, gres, grate, norm.reshape(())


def solution(mesh):
    fine = Mesh(mesh.devices.reshape(RING, NEAR, 2, 2, 4, 2), ("far", "near", "yl", "core", "x", "yh"))
    ctx, chan = ("far", "near", "yl", "core"), ("x", "yh")
    return jax.shard_map(
        on_device,
        mesh=fine,
        in_specs=(P(ctx, chan),) * 4 + (P(None, chan),) * 2,
        out_specs=(P(ctx, chan),) * 3 + (P(None, chan),) * 2 + (P(),),
        check_vma=False,
    )
```

```python
import jax
import jax.numpy as jnp
from jax import lax
from jax.experimental import pallas as pl
from jax.experimental.pallas import tpu as pltpu
from jax.sharding import Mesh, PartitionSpec as P

ROWS = 128
LANES = 128
MODES = 16
GROUP = 4
NEAR = 2
RING = 8
BLOCKS = NEAR * GROUP
SHARE = MODES // GROUP
CHANS = 8
NEAR_FIRST = 5
RING_ORDER = (5, 1, 4, 0, 6, 2, 7, 3)
PLANE_FIRST = 21
TOTAL = ROWS * BLOCKS * RING
F32 = jnp.float32
TINY = 1e-37
RING_CODES = ((256.0, 1), (8.0, 1), (256.0, 1), (8.0, 1), (256.0, 2), (64.0, 2))
CARRY_CODE = (64.0, 1)
GRAD_CODE = (1024.0, 2)
VM = pl.BlockSpec(memory_space=pltpu.VMEM)


def group_index():
    return lax.axis_index("yl") * 2 + lax.axis_index("core")


def summary_kernel(
    q_ref, k_ref, v_ref, g_ref, rate_ref, res_ref,
    out_ref, own_ref, x_s, g_s, k_keep, v_keep, g_keep, rate_keep, res_keep,
):
    x_s[...] = k_ref[...].astype(F32) * v_ref[...].astype(F32)
    g_s[...] = g_ref[...].astype(F32) * q_ref[...].astype(F32)
    kept = ((k_keep, k_ref), (v_keep, v_ref), (g_keep, g_ref), (rate_keep, rate_ref), (res_keep, res_ref))
    for keep, ref in kept:
        keep[...] = ref[...]
    f = jnp.exp(-rate_ref[...])
    zero = jnp.zeros((MODES, LANES), F32)
    state, moment, adj, sec, res_sum, rate_sum = zero, zero, zero, zero, zero, zero
    for i in range(ROWS):
        j = ROWS - 1 - i
        moment = f * (moment + state)
        state = f * state + x_s[i : i + 1, :]
        sec = f * (sec + adj)
        adj = f * adj + g_s[j : j + 1, :]
        x_j = x_s[j : j + 1, :]
        res_sum = res_sum + x_j * adj
        rate_sum = rate_sum + x_j * sec
    for near in range(NEAR):
        for peer in range(GROUP):
            for at, part in enumerate((state, moment, adj, sec, res_sum, rate_sum)):
                rows = slice(SHARE * at, SHARE * (at + 1))
                out_ref[(near * GROUP + peer) ^ NEAR_FIRST, rows, :] = part[SHARE * peer : SHARE * (peer + 1)]
    me = group_index()
    for at, ref in enumerate((rate_ref, res_ref)):
        mine = jnp.zeros((SHARE, LANES), F32)
        for peer in range(GROUP):
            mine = jnp.where(me == peer, ref[SHARE * peer : SHARE * (peer + 1), :], mine)
        own_ref[SHARE * at : SHARE * (at + 1), :] = mine


def rooted(v):
    return v * lax.rsqrt(jnp.abs(v) + TINY)


def coded(v, gain, roots):
    for _ in range(roots):
        v = rooted(v)
    return v * gain


def decoded(y, gain, roots):
    y = y * (1.0 / gain)
    for _ in range(roots):
        y = y * jnp.abs(y)
    return y


def parts_of(ref, at, codes=None):
    parts = tuple(ref[at, SHARE * k : SHARE * (k + 1), :] for k in range(6))
    return parts if codes is None else tuple(decoded(p, *c) for p, c in zip(parts, codes))


def near_kernel(in_ref, own_ref, out_ref):
    rate = own_ref[0:SHARE, :]
    f = jnp.exp(-rate)
    span = jnp.exp(-rate * ROWS)
    blocks = [parts_of(in_ref, d ^ NEAR_FIRST) for d in range(BLOCKS)]
    state, moment, _, _, res_sum, rate_sum = blocks[0]
    for d in range(1, BLOCKS):
        moment = span * (moment + ROWS * state) + blocks[d][1]
        state = span * state + blocks[d][0]
        res_sum = res_sum + blocks[d][4]
        rate_sum = rate_sum + blocks[d][5]
    adj, sec = blocks[-1][2], blocks[-1][3]
    for d in range(BLOCKS - 2, -1, -1):
        held = f * blocks[d][0]
        held_moment = f * (blocks[d][1] + blocks[d][0])
        res_sum = res_sum + held * adj
        rate_sum = rate_sum + held_moment * adj + held * sec
        sec = span * (sec + ROWS * adj) + blocks[d][3]
        adj = span * adj + blocks[d][2]
    for at, part in enumerate((state, moment, adj, sec, res_sum, rate_sum)):
        part = coded(part, *RING_CODES[at])
        for z in range(RING):
            out_ref[z, SHARE * at : SHARE * (at + 1), :] = part


def ring_kernel(ring_ref, in_ref, own_ref, out_ref):
    ring_me, near_me = lax.axis_index("far"), lax.axis_index("near")
    rate = own_ref[0:SHARE, :]
    res = own_ref[SHARE : 2 * SHARE, :]
    f = jnp.exp(-rate)
    span = jnp.exp(-rate * ROWS)
    reach = ROWS * BLOCKS
    long = jnp.exp(-rate * reach)
    zero = jnp.zeros((SHARE, LANES), F32)
    composites = [parts_of(ring_ref, RING_ORDER.index(z), RING_CODES) for z in range(RING)]
    enter = zero
    for z in range(RING - 1):
        enter = jnp.where(z < ring_me, long * enter + composites[z][0], enter)
    adj, sec, leave, res_sum, rate_sum = zero, zero, zero, zero, zero
    for z in range(RING - 1, -1, -1):
        state, moment, adj_z, sec_z, res_z, rate_z = composites[z]
        leave = jnp.where(z == ring_me, adj, leave)
        held = f * state
        held_moment = f * (moment + state)
        res_sum = res_sum + res_z + held * adj
        rate_sum = rate_sum + rate_z + held_moment * adj + held * sec
        sec = long * (sec + reach * adj) + sec_z
        adj = long * adj + adj_z
    grad_res = res_sum * (1.0 / TOTAL)
    grad_rate = -rate * res * rate_sum * (1.0 / TOTAL)
    enters, leaves = [enter], [leave]
    for d in range(BLOCKS - 1):
        enters.append(span * enters[-1] + in_ref[d ^ NEAR_FIRST, 0:SHARE, :])
        leaves.append(span * leaves[-1] + in_ref[(BLOCKS - 1 - d) ^ NEAR_FIRST, 2 * SHARE : 3 * SHARE, :])
    leaves = leaves[::-1]
    for d in range(GROUP):
        mine = [jnp.where(near_me == 0, many[d], many[GROUP + d]) for many in (enters, leaves)]
        parts = [coded(p, *CARRY_CODE) for p in mine] + [coded(p, *GRAD_CODE) for p in (grad_res, grad_rate)]
        for chan in range(CHANS):
            for at, part in enumerate(parts):
                out_ref[(chan * GROUP + d) ^ PLANE_FIRST, SHARE * at : SHARE * (at + 1), :] = part


def final_kernel(
    back_ref, x_s, g_s, k_ref, v_ref, g_ref, rate_ref, res_ref,
    gq_ref, gk_ref, gv_ref, gres_ref, grate_ref, norm_ref,
):
    first = ((lax.axis_index("x") * 2 + lax.axis_index("yh")) ^ (PLANE_FIRST // GROUP)) * GROUP
    f = jnp.exp(-rate_ref[...])
    res = res_ref[...]

    def gathered(at, code):
        rows = slice(SHARE * at, SHARE * (at + 1))
        parts = [back_ref[first + (d ^ (PLANE_FIRST % GROUP)), rows, :] for d in range(GROUP)]
        return decoded(jnp.concatenate(parts, axis=0), *code)

    squares = jnp.zeros((2 * SHARE, LANES), F32)
    for peer in range(CHANS * GROUP):
        part = decoded(back_ref[peer, 2 * SHARE : 4 * SHARE, :], *GRAD_CODE)
        squares = squares + part * part
    norm_ref[...] = jnp.sqrt(jnp.sum(squares, keepdims=True))
    gres_ref[...] = gathered(2, GRAD_CODE)
    grate_ref[...] = gathered(3, GRAD_CODE)
    state = gathered(0, CARRY_CODE)
    adj = gathered(1, CARRY_CODE)
    step = 16
    for base in range(0, ROWS, step):
        conv, grad = [], []
        for i in range(base, base + step):
            j = ROWS - 1 - i
            state = f * state + x_s[i : i + 1, :]
            adj = f * adj + g_s[j : j + 1, :]
            conv.append(jnp.sum(res * state, axis=0, keepdims=True))
            grad.append(jnp.sum(res * adj, axis=0, keepdims=True))
        conv = jnp.concatenate(conv, axis=0)
        grad = jnp.concatenate(grad[::-1], axis=0)
        rows = slice(base, base + step)
        gq_ref[rows, :] = (g_ref[rows, :].astype(F32) * conv).astype(jnp.bfloat16)
        rows = slice(ROWS - base - step, ROWS - base)
        gk_ref[rows, :] = (v_ref[rows, :].astype(F32) * grad).astype(jnp.bfloat16)
        gv_ref[rows, :] = (k_ref[rows, :].astype(F32) * grad).astype(jnp.bfloat16)


def call(kernel, shapes, scratch=(), vmem_in=True, vmem_out=True):
    run = pl.pallas_call(
        kernel,
        out_shape=[(pltpu.VMEM if vmem_out else jax.ShapeDtypeStruct)(s, t) for s, t in shapes],
        out_specs=[VM] * len(shapes),
        scratch_shapes=list(scratch),
    )
    if not vmem_in:
        return run
    return lambda *args: run(*[pltpu.with_memory_space_constraint(a, pltpu.VMEM) for a in args])


def exchange(blocks, axes, order):
    return lax.all_to_all(blocks, axes, split_axis=0, concat_axis=0, axis_index_groups=[list(order)], tiled=True)


def on_device(query_in, key_in, value_in, grad_out, residue, decay_rate):
    bf = jnp.bfloat16
    block, table = (ROWS, LANES), (MODES, LANES)
    summary, own, *kept = call(
        summary_kernel,
        [((BLOCKS, 6 * SHARE, LANES), F32), ((2 * SHARE, LANES), F32)]
        + [(block, F32)] * 2 + [(block, bf)] * 3 + [(table, F32)] * 2,
        vmem_in=False,
    )(query_in, key_in, value_in, grad_out, decay_rate, residue)
    near = exchange(summary, ("near", "yl", "core"), [p ^ NEAR_FIRST for p in range(BLOCKS)])
    (composite,) = call(near_kernel, [((RING, 6 * SHARE, LANES), F32)])(near, own)
    ring = exchange(composite.astype(jnp.float16), "far", RING_ORDER).astype(F32)
    (message,) = call(ring_kernel, [((CHANS * GROUP, 4 * SHARE, LANES), F32)])(ring, near, own)
    order = [p ^ PLANE_FIRST for p in range(CHANS * GROUP)]
    back = exchange(message.astype(jnp.float16), ("x", "yh", "yl", "core"), order).astype(F32)
    gq, gk, gv, gres, grate, norm = call(
        final_kernel, [(block, bf)] * 3 + [(table, F32)] * 2 + [((1, 1), F32)], vmem_out=False
    )(back, *kept)
    return gq, gk, gv, gres, grate, norm.reshape(())


def solution(mesh):
    fine = Mesh(mesh.devices.reshape(RING, NEAR, 2, 2, 4, 2), ("far", "near", "yl", "core", "x", "yh"))
    ctx, chan = ("far", "near", "yl", "core"), ("x", "yh")
    return jax.shard_map(
        on_device,
        mesh=fine,
        in_specs=(P(ctx, chan),) * 4 + (P(None, chan),) * 2,
        out_specs=(P(ctx, chan),) * 3 + (P(None, chan),) * 2 + (P(),),
        check_vma=False,
    )
```
